32 devices in a mesh: groups: 2 (over x), mp: 8 (over z, y), dp: 2 (over core).
Axes of the slice: x: 2, y: 2, z: 4, core: 2. Of those that a mesh axis runs over, the one named last changes fastest.
Arguments:
- latents: bfloat16 [12, 128, 128, 320], P(('groups', 'dp'), 'mp'), parts along dimension 0, may hold values from -6 to 6
- room_labels: int32 [12, 128, 128], P(('groups', 'dp'), 'mp'), parts along dimension 0, may hold values from 0 to 15
- timesteps: int32 [12], P(('groups', 'dp')), parts along dimension 0, may hold values from 0 to 999
- label_table: bfloat16 [16, 320], replicated, may hold values from -6 to 6
- time_weight: bfloat16 [1280, 320], replicated, may hold values from -0.15625 to 0.15625
- trunk_weight: bfloat16 [320, 3, 3, 320], P('mp'), may hold values from -0.109375 to 0.109375
- control_weight: bfloat16 [320, 3, 3, 320], P('mp'), may hold values from -0.109375 to 0.109375
- mix_weight: bfloat16 [320, 320], P('mp'), may hold values from -0.3125 to 0.3125
- cotangent: bfloat16 [12, 128, 128, 320], P(('groups', 'dp'), 'mp'), parts along dimension 0, may hold values from -0.08984375 to 0.08984375
Outputs:
- output: bfloat16 [12, 128, 128, 320], P(('groups', 'dp'), 'mp'), parts along dimension 0
- grad_control: float32 [640, 3, 3, 320], P(('groups', 'mp')), parts along dimension 0
- grad_mix: float32 [640, 320], P(('groups', 'mp')), parts along dimension 0
- grad_table: float32 [32, 320], P('groups'), parts along dimension 0
The draws below stay inside these ranges and needn't reach their ends.
There are 2 independent parts, one for each index of `groups`. The reference program is written for one: setup_inputs(seed, part) draws one part's arguments, and reference() takes and returns one part's arrays. A program takes and returns all parts, laid end to end along the dimension named above; an argument that names none is the same for every part. Nothing has to cross between parts.
All inputs are finite; a program needn't handle non-finite values.
Results may differ from the reference program's by a relative error of at most 0.0057.
Values may be sent and summed in bfloat16 or wider, within the bound.
A program may use at most 256 MiB of HBM per device.

```python
import math
import jax
import jax.numpy as jnp

C = 320
H = 128
W = 128
TEMB = 1280
ROOMS = 16
IMAGES = 6


def touch_ends(result, rng, least, high):
    longest = result.shape.index(max(result.shape))
    spots = []
    for shift in (0, 1):
        where = [jax.random.randint(jax.random.fold_in(rng, axis), (), 0, length) for axis, length in enumerate(result.shape)]
        where[longest] = (where[longest] + shift) % result.shape[longest]
        spots.append(tuple(where))
    return result.at[spots[0]].set(least).at[spots[1]].set(high)


def shard_levels(key, dims, cuts, smallest, high):
    def one(axis_at, parts):
        heights = jax.random.uniform(jax.random.fold_in(jax.random.fold_in(key, 6), axis_at), (parts,), jnp.float32, smallest / len(cuts), high / len(cuts))
        return jnp.repeat(jnp.exp(heights), dims[axis_at] // parts).reshape((-1,) + (1,) * (len(dims) - axis_at - 1))

    gain = one(*cuts[0])
    for cut in cuts[1:]:
        gain = gain * one(*cut)
    return gain


def noise(stream_key, extent, spread, most, cuts=(), held_as=jnp.bfloat16):
    level = shard_levels(stream_key, extent, cuts, -0.22, 0.18) if cuts else 1.0
    result = jax.random.normal(stream_key, extent, jnp.float32) * spread * level
    return jnp.minimum(jnp.maximum(result, -most), most).astype(held_as)


def setup_inputs(seed: int = 0, part: int = 0) -> dict:
    key_of = jax.random.split(jax.random.key(seed), 10)
    part_splits = jax.random.split(jax.random.fold_in(key_of[9], part), 10)
    latents = noise(part_splits[0], (IMAGES, H, W, C), 1.0, 6.0, ((0, 2), (1, 8)))
    room_labels = touch_ends(jax.random.randint(part_splits[1], (IMAGES, H, W), 0, ROOMS), jax.random.fold_in(part_splits[1], 1), 0, ROOMS - 1).astype(jnp.int32)
    timesteps = touch_ends(jax.random.randint(part_splits[2], (IMAGES,), 0, 1000), jax.random.fold_in(part_splits[2], 1), 0, 999).astype(jnp.int32)
    label_table = noise(key_of[3], (ROOMS, C), 1.0, 6.0)
    time_weight = noise(key_of[4], (TEMB, C), TEMB ** -0.5, 0.15625)
    trunk_weight = noise(key_of[5], (C, 3, 3, C), (9 * C) ** -0.5, 0.109375, ((0, 8),))
    control_weight = noise(key_of[6], (C, 3, 3, C), (9 * C) ** -0.5, 0.109375, ((0, 8),))
    mix_weight = noise(key_of[7], (C, C), C ** -0.5, 0.3125, ((0, 8),))
    cotangent = noise(part_splits[8], (IMAGES, H, W, C), 0.015625, 0.08984375, ((0, 2), (1, 8)))
    return dict(latents=latents, room_labels=room_labels, timesteps=timesteps, label_table=label_table, time_weight=time_weight, trunk_weight=trunk_weight, control_weight=control_weight, mix_weight=mix_weight, cotangent=cotangent)


def sinusoid(timesteps):
    half_width = TEMB // 2
    indices = jnp.arange(half_width, dtype=jnp.float32)
    frequency = jnp.exp(-math.log(10000.0) * indices / half_width)
    angles = timesteps.astype(jnp.float32)[:, None] * frequency[None, :]
    return jnp.concatenate([jnp.cos(angles), jnp.sin(angles)], axis=1)

def convolve(inputs, kernel):
    padded = jnp.pad(inputs, ((0, 0), (1, 1), (1, 1), (0, 0))).astype(jnp.float32)
    kernel_wide = kernel.astype(jnp.float32)
    running = jnp.zeros(inputs.shape[:3] + (kernel.shape[3],), jnp.float32)
    for tap_row in range(3):
        for tap_col in range(3):
            running = running + jnp.einsum('bhwc,cd->bhwd', padded[:, tap_row:tap_row + H, tap_col:tap_col + W], kernel_wide[:, tap_row, tap_col])
    return running

def transposed(grads, kernel):
    padded = jnp.pad(grads, ((0, 0), (1, 1), (1, 1), (0, 0))).astype(jnp.float32)
    kernel_wide = kernel.astype(jnp.float32)
    running = jnp.zeros(grads.shape[:3] + (kernel.shape[0],), jnp.float32)
    for tap_row in range(3):
        for tap_col in range(3):
            running = running + jnp.einsum('bhwd,cd->bhwc', padded[:, 2 - tap_row:2 - tap_row + H, 2 - tap_col:2 - tap_col + W], kernel_wide[:, tap_row, tap_col])
    return running

def kernel_grad(inputs, grads):
    padded = jnp.pad(inputs, ((0, 0), (1, 1), (1, 1), (0, 0))).astype(jnp.float32)
    grads_wide = grads.astype(jnp.float32)
    pieces = []
    for tap_row in range(3):
        for tap_col in range(3):
            pieces.append(jnp.einsum('bhwc,bhwd->cd', padded[:, tap_row:tap_row + H, tap_col:tap_col + W], grads_wide))
    return jnp.stack(pieces, axis=1).reshape(C, 3, 3, C)

def reference(latents, room_labels, timesteps, label_table, time_weight, trunk_weight, control_weight, mix_weight, cotangent):
    time_features = jax.nn.silu(sinusoid(timesteps)).astype(jnp.bfloat16)
    time_shift = jnp.dot(time_features, time_weight, preferred_element_type=jnp.float32)[:, None, None, :]
    control_in = (latents.astype(jnp.float32) + label_table[room_labels].astype(jnp.float32)).astype(jnp.bfloat16)
    trunk_pre = convolve(latents, trunk_weight) + time_shift
    control_pre = convolve(control_in, control_weight) + time_shift
    gated = jax.nn.silu(control_pre).astype(jnp.bfloat16)
    mixed_out = jnp.einsum('bhwc,cd->bhwd', gated.astype(jnp.float32), mix_weight.astype(jnp.float32))
    output = (jax.nn.silu(trunk_pre) + mixed_out).astype(jnp.bfloat16)
    grad_mix = jnp.einsum('bhwc,bhwd->cd', gated.astype(jnp.float32), cotangent.astype(jnp.float32))
    back_gate = jnp.einsum('bhwd,cd->bhwc', cotangent.astype(jnp.float32), mix_weight.astype(jnp.float32))
    sigmoid_val = jax.nn.sigmoid(control_pre)
    back_pre = (back_gate * sigmoid_val * (1.0 + control_pre * (1.0 - sigmoid_val))).astype(jnp.bfloat16)
    grad_control = kernel_grad(control_in, back_pre)
    back_in = transposed(back_pre, control_weight)
    grad_table = jax.ops.segment_sum(back_in.reshape(-1, C), room_labels.reshape(-1).astype(jnp.int32), num_segments=ROOMS)
    return (output, grad_control, grad_mix, grad_table)
```

```python
import functools
import math

import jax
import jax.numpy as jnp
from jax import lax
from jax.experimental import pallas as pl
from jax.experimental.pallas import tpu as pltpu
from jax.sharding import PartitionSpec as P

MESH = pl.DeviceIdType.MESH
LANES = 128
MIB = 1024 * 1024


def ring_position(index, count):
    if count != 8:
        return index
    short, long = index % 2, index // 2
    return (1 - short) * long + short * (count - 1 - long)


def ring_index(position, count):
    if count != 8:
        return position
    short = position // (count // 2)
    long = (1 - short) * position + short * (count - 1 - position)
    return 2 * long + short


def signal_all(targets):
    barrier = pltpu.get_barrier_semaphore()
    for target in targets:
        pl.semaphore_signal(barrier, inc=1, device_id=target, device_id_type=MESH)
    pl.semaphore_wait(barrier, len(targets))


def gather_kernel(n, w_ref, f_ref, g_ref, halo_ref, ring_send, ring_recv, sib_send, sib_recv, halo_send, halo_recv, own_sem):
    me = lax.axis_index("mp")
    core = lax.axis_index("dp")
    pos = ring_position(me, n)
    right = {"mp": ring_index((pos + 1) % n, n)}
    left = {"mp": ring_index((pos + n - 1) % n, n)}
    up = {"mp": (me + n - 1) % n}
    down = {"mp": (me + 1) % n}
    sibling = {"dp": 1 - core}
    signal_all((right, left, up, down, sibling))
    half = w_ref.shape[0] // 2
    mine = pl.ds(core * half, half)
    rows = f_ref.shape[1]

    def remote(src, dst, send, recv, target):
        return pltpu.make_async_remote_copy(
            src_ref=src, dst_ref=dst, send_sem=send, recv_sem=recv, device_id=target, device_id_type=MESH
        )

    right_steps = n // 2
    left_steps = n - 1 - right_steps
    pending = []
    ring = {}

    def send(side, step):
        shift = n - step if side == 0 else step
        origin = ring_index((pos + shift) % n, n)
        src = w_ref.at[mine] if step == 0 else g_ref.at[origin, mine]
        slot = side * right_steps + step
        copy = remote(src, g_ref.at[origin, mine], ring_send.at[slot], ring_recv.at[slot], (right, left)[side])
        copy.start()
        ring[side, step] = copy

    send(0, 0)
    if left_steps:
        send(1, 0)
    halo_down = remote(f_ref.at[:, rows - 1], halo_ref.at[0], halo_send.at[0], halo_recv.at[0], down)
    halo_up = remote(f_ref.at[:, 0], halo_ref.at[1], halo_send.at[1], halo_recv.at[1], up)
    halo_down.start()
    halo_up.start()
    own = pltpu.make_async_copy(w_ref, g_ref.at[me], own_sem)
    own.start()
    for step in range(right_steps):
        for side, steps in ((0, right_steps), (1, left_steps)):
            if step >= steps:
                continue
            ring[side, step].wait_recv()
            if step + 1 < steps:
                send(side, step + 1)
            shift = n - step - 1 if side == 0 else step + 1
            origin = ring_index((pos + shift) % n, n)
            slot = side * right_steps + step
            copy = remote(
                g_ref.at[origin, mine], g_ref.at[origin, mine], sib_send.at[slot], sib_recv.at[slot], sibling
            )
            copy.start()
            pending.append(copy)
    for copy in ring.values():
        copy.wait_send()
    for copy in pending:
        copy.wait()
    halo_down.wait()
    halo_up.wait()
    own.wait()


def gather(n, w, f):
    images, _, cols, lanes = f.shape
    return pl.pallas_call(
        functools.partial(gather_kernel, n),
        out_shape=(
            jax.ShapeDtypeStruct((n,) + w.shape, w.dtype),
            jax.ShapeDtypeStruct((2, images, cols, lanes), f.dtype),
        ),
        in_specs=[pl.BlockSpec(memory_space=pl.ANY)] * 2,
        out_specs=(pl.BlockSpec(memory_space=pl.ANY),) * 2,
        scratch_shapes=[
            pltpu.SemaphoreType.DMA((n,)),
            pltpu.SemaphoreType.DMA((n,)),
            pltpu.SemaphoreType.DMA((n,)),
            pltpu.SemaphoreType.DMA((n,)),
            pltpu.SemaphoreType.DMA((2,)),
            pltpu.SemaphoreType.DMA((2,)),
            pltpu.SemaphoreType.DMA,
        ],
        compiler_params=pltpu.CompilerParams(collective_id=0, has_side_effects=True),
        name="gather",
    )(w, f)


def compute_kernel(
    n, rows, chunks, lanes, channels, rooms,
    main_ref, prev_ref, next_ref, top_ref, bottom_ref, shift_ref, w_ref, mix_ref, mixt_ref, table_ref, tablet_ref, cot_ref,
    out_ref, parts_ref, gtable_ref,
    cols_ref, wide_ref, grad_ref, gmix_ref,
):
    image = pl.program_id(0)
    chunk = pl.program_id(1)
    first = jnp.logical_and(image == 0, chunk == 0)
    last = jnp.logical_and(image == pl.num_programs(0) - 1, chunk == chunks - 1)
    span = main_ref.shape[2]

    @pl.when(first)
    def _():
        wide_ref[...] = jnp.zeros_like(wide_ref)
        grad_ref[...] = jnp.zeros_like(grad_ref)
        gmix_ref[...] = jnp.zeros_like(gmix_ref)
        for tap in range(9):
            base = tap * lanes
            control = w_ref[10 + tap]
            wide_ref[base : base + channels, 0:channels] = w_ref[tap]
            wide_ref[base : base + channels, lanes : lanes + channels] = control
            wide_ref[base + channels : base + channels + rooms, lanes : lanes + channels] = jnp.dot(
                table_ref[...], control, preferred_element_type=jnp.float32
            ).astype(jnp.bfloat16)

    above = jnp.where(chunk == 0, top_ref[0], prev_ref[0, 0])
    below = jnp.where(chunk == chunks - 1, bottom_ref[0], next_ref[0, 0])
    spot = lax.broadcasted_iota(jnp.int32, (span, lanes), 0)
    for row in range(rows + 2):
        if row == 0:
            here = above
        elif row == rows + 1:
            here = below
        else:
            here = main_ref[0, row - 1]
        wide = here.astype(jnp.float32)
        shifted = (
            jnp.where(spot == 0, 0.0, pltpu.roll(wide, 1, 0)).astype(jnp.bfloat16),
            here,
            jnp.where(spot == span - 1, 0.0, pltpu.roll(wide, span - 1, 0)).astype(jnp.bfloat16),
        )
        for tap_row in range(3):
            spot_row = row - tap_row
            if 0 <= spot_row < rows:
                for tap_col in range(3):
                    base = (tap_row * 3 + tap_col) * lanes
                    cols_ref[spot_row * span : (spot_row + 1) * span, base : base + lanes] = shifted[tap_col]

    cells = rows * span
    cot = cot_ref[0].reshape(cells, channels)
    pre = jnp.dot(cols_ref[...], wide_ref[...], preferred_element_type=jnp.float32)
    shift = shift_ref[0]
    trunk = pre[:, :lanes] + shift
    control = pre[:, lanes:] + shift
    gate = 0.5 + 0.5 * jnp.tanh(0.5 * control)
    gated = (control * gate).astype(jnp.bfloat16)
    back = jnp.dot(cot, mixt_ref[...], preferred_element_type=jnp.float32)
    back_pre = (back * gate * (1.0 + control * (1.0 - gate))).astype(jnp.bfloat16)
    mixed = jnp.dot(gated, mix_ref[...], preferred_element_type=jnp.float32)
    trunk = trunk * (0.5 + 0.5 * jnp.tanh(0.5 * trunk))
    out = trunk[:, :channels] + mixed
    out_ref[0] = out.astype(jnp.bfloat16).reshape(rows, span, channels)
    back_t = back_pre.T[:channels]
    gated_t = gated.T[:channels]
    gmix_ref[...] += jnp.dot(gated_t, cot, preferred_element_type=jnp.float32)
    for tap_row in range(3):
        base = tap_row * 3 * lanes
        grad_ref[:, base : base + 3 * lanes] += jnp.dot(
            back_t, cols_ref[:, base : base + 3 * lanes], preferred_element_type=jnp.float32
        )

    @pl.when(last)
    def _():
        share = channels // n

        def put(tap, block):
            for owner in range(n):
                parts_ref[owner, tap] = block[owner * share : (owner + 1) * share].astype(parts_ref.dtype)

        total = jnp.zeros((2 * rooms, channels), jnp.float32)
        for tap in range(9):
            base = tap * lanes
            block = grad_ref[:, base : base + lanes].T
            room = block[channels : channels + rooms]
            high = room.astype(jnp.bfloat16)
            low = (room - high.astype(jnp.float32)).astype(jnp.bfloat16)
            pair = jnp.concatenate([high, low], axis=0)
            put(tap, block[:channels] + jnp.dot(tablet_ref[...], pair, preferred_element_type=jnp.float32))
            total = total + lax.dot_general(
                pair, w_ref[10 + tap], (((1,), (1,)), ((), ())), preferred_element_type=jnp.float32
            )
        put(9, gmix_ref[...])
        gtable_ref[...] = total[:rooms] + total[rooms:]


def compute(n, frame, top, bottom, shift, weights, mix, mixt, table, cotangent, rows):
    images, height, span, lanes = frame.shape
    channels = cotangent.shape[3]
    rooms = table.shape[0]
    chunks = height // rows
    tablet = jnp.concatenate([table.T, table.T], axis=1)

    def whole(array):
        return pl.BlockSpec(array.shape, lambda b, h: (0,) * array.ndim, pipeline_mode=pl.Buffered(1))

    return pl.pallas_call(
        functools.partial(compute_kernel, n, rows, chunks, lanes, channels, rooms),
        grid=(images, chunks),
        out_shape=(
            jax.ShapeDtypeStruct((images, height, span, channels), jnp.bfloat16),
            jax.ShapeDtypeStruct((n, 10, channels // n, channels), jnp.bfloat16),
            jax.ShapeDtypeStruct((rooms, channels), jnp.float32),
        ),
        in_specs=[
            pl.BlockSpec((1, rows, span, lanes), lambda b, h: (b, h, 0, 0)),
            pl.BlockSpec((1, 1, span, lanes), lambda b, h: (b, jnp.maximum(h * rows - 1, 0), 0, 0)),
            pl.BlockSpec((1, 1, span, lanes), lambda b, h: (b, jnp.minimum((h + 1) * rows, height - 1), 0, 0)),
            pl.BlockSpec((1, span, lanes), lambda b, h: (b, 0, 0)),
            pl.BlockSpec((1, span, lanes), lambda b, h: (b, 0, 0)),
            pl.BlockSpec((1, 1, lanes), lambda b, h: (b, 0, 0)),
            whole(weights),
            whole(mix),
            whole(mixt),
            whole(table),
            whole(tablet),
            pl.BlockSpec((1, rows, span, channels), lambda b, h: (b, h, 0, 0)),
        ],
        out_specs=(
            pl.BlockSpec((1, rows, span, channels), lambda b, h: (b, h, 0, 0)),
            pl.BlockSpec((n, 10, channels // n, channels), lambda b, h: (0, 0, 0, 0), pipeline_mode=pl.Buffered(1)),
            pl.BlockSpec((rooms, channels), lambda b, h: (0, 0)),
        ),
        scratch_shapes=[
            pltpu.VMEM((rows * span, 9 * lanes), jnp.bfloat16),
            pltpu.VMEM((9 * lanes, 2 * lanes), jnp.bfloat16),
            pltpu.VMEM((channels, 9 * lanes), jnp.float32),
            pltpu.VMEM((channels, channels), jnp.float32),
        ],
        compiler_params=pltpu.CompilerParams(vmem_limit_bytes=56 * MIB),
        cost_estimate=pl.CostEstimate(flops=60 * 10**9, bytes_accessed=20 * 10**6, transcendentals=4 * 10**6),
        name="convolve",
    )(frame, frame, frame, top, bottom, shift, weights, mix, mixt, table, tablet, cotangent)


def reduce_kernel(n, parts_ref, out_ref, other, inbox, outbox, final, pair_sems, send_sems, recv_sems, last_sems):
    me = lax.axis_index("mp")
    core = lax.axis_index("dp")
    pos = ring_position(me, n)
    right = {"mp": ring_index((pos + 1) % n, n)}
    left = {"mp": ring_index((pos + n - 1) % n, n)}
    sibling = {"dp": 1 - core}
    signal_all((right, left, sibling))
    half = parts_ref.shape[1] // 2
    mine = pl.ds(core * half, half)
    theirs = pl.ds((1 - core) * half, half)

    def remote(src, dst, send, recv, target):
        return pltpu.make_async_remote_copy(
            src_ref=src, dst_ref=dst, send_sem=send, recv_sem=recv, device_id=target, device_id_type=MESH
        )

    right_steps = n // 2
    left_steps = n - 1 - right_steps
    order = []
    for step in range(right_steps):
        order.append((0, step))
        if step < left_steps:
            order.append((1, step))

    def goal(side, step):
        if side == 0:
            return ring_index((pos + right_steps - step) % n, n)
        return ring_index((pos + n - left_steps + step) % n, n)

    pairs = {}
    for spot, key in enumerate(order + [None]):
        owner = me if key is None else goal(*key)
        copy = remote(
            parts_ref.at[owner, theirs], other.at[owner], pair_sems.at[0, spot], pair_sems.at[1, spot], sibling
        )
        copy.start()
        pairs[key] = copy

    ring = {}
    for side, step in order:
        owner = goal(side, step)
        pairs[side, step].wait_recv()
        total = parts_ref[owner, mine].astype(jnp.float32) + other[owner].astype(jnp.float32)
        slot = side * right_steps + step
        if step:
            ring[side, step - 1].wait_recv()
            total = total + inbox[slot - 1].astype(jnp.float32)
        outbox[slot] = total.astype(outbox.dtype)
        copy = remote(
            outbox.at[slot], inbox.at[slot], send_sems.at[slot], recv_sems.at[slot], (right, left)[side]
        )
        copy.start()
        ring[side, step] = copy
    pairs[None].wait_recv()
    total = parts_ref[me, mine].astype(jnp.float32) + other[me].astype(jnp.float32)
    for side, steps in ((1, left_steps), (0, right_steps)):
        if steps:
            ring[side, steps - 1].wait_recv()
            total = total + inbox[side * right_steps + steps - 1].astype(jnp.float32)
    final[...] = total
    swap = remote(final, out_ref.at[mine], last_sems.at[0], last_sems.at[1], sibling)
    swap.start()
    keep = pltpu.make_async_copy(final, out_ref.at[mine], last_sems.at[2])
    keep.start()
    for copy in pairs.values():
        copy.wait_send()
    for copy in ring.values():
        copy.wait_send()
    keep.wait()
    swap.wait()


def reduce(n, parts):
    _, count, share, channels = parts.shape
    half = count // 2
    return pl.pallas_call(
        functools.partial(reduce_kernel, n),
        out_shape=jax.ShapeDtypeStruct((count, share, channels), jnp.float32),
        in_specs=[pl.BlockSpec(memory_space=pltpu.VMEM)],
        out_specs=pl.BlockSpec(memory_space=pl.ANY),
        scratch_shapes=[
            pltpu.VMEM((n, half, share, channels), jnp.bfloat16),
            pltpu.VMEM((n, half, share, channels), jnp.bfloat16),
            pltpu.VMEM((n, half, share, channels), jnp.bfloat16),
            pltpu.VMEM((half, share, channels), jnp.float32),
            pltpu.SemaphoreType.DMA((2, n)),
            pltpu.SemaphoreType.DMA((n,)),
            pltpu.SemaphoreType.DMA((n,)),
            pltpu.SemaphoreType.DMA((3,)),
        ],
        compiler_params=pltpu.CompilerParams(
            collective_id=1, has_side_effects=True, vmem_limit_bytes=40 * MIB
        ),
        cost_estimate=pl.CostEstimate(flops=10**9, bytes_accessed=50 * 10**6, transcendentals=0),
        name="scatter",
    )(parts)


def sinusoid(timesteps, embed_width):
    half_width = embed_width // 2
    indices = jnp.arange(half_width, dtype=jnp.float32)
    frequency = jnp.exp(-math.log(10000.0) * indices / half_width)
    angles = timesteps.astype(jnp.float32)[:, None] * frequency[None, :]
    return jnp.concatenate([jnp.cos(angles), jnp.sin(angles)], axis=1)


def per_device(
    n,
    latents,
    room_labels,
    timesteps,
    label_table,
    time_weight,
    trunk_weight,
    control_weight,
    mix_weight,
    cotangent,
):
    images, height, span, channels = latents.shape
    rooms = label_table.shape[0]
    share = trunk_weight.shape[0]
    lanes = -(-(channels + rooms) // LANES) * LANES
    onehot = (room_labels[..., None] == jnp.arange(lanes - channels, dtype=jnp.int32)).astype(jnp.bfloat16)
    frame = jnp.concatenate([latents, onehot], axis=-1)

    def by_tap(weight):
        return weight.reshape(share, 9, channels).transpose(1, 0, 2)

    packed = jnp.concatenate(
        [by_tap(trunk_weight), mix_weight[None], by_tap(control_weight), mix_weight[None]], axis=0
    )
    gathered, halo = gather(n, packed, frame)
    weights = gathered.transpose(1, 0, 2, 3).reshape(20, n * share, channels)
    me = lax.axis_index("mp")
    top = jnp.where(me == 0, 0, halo[0])
    bottom = jnp.where(me == n - 1, 0, halo[1])
    time_features = jax.nn.silu(sinusoid(timesteps, time_weight.shape[0])).astype(jnp.bfloat16)
    time_shift = jnp.dot(time_features, time_weight, preferred_element_type=jnp.float32)
    time_shift = jnp.pad(time_shift, ((0, 0), (0, lanes - channels)))[:, None, :]
    mix = jnp.pad(weights[9], ((0, lanes - channels), (0, 0)))
    output, parts, table_local = compute(
        n, frame, top, bottom, time_shift, weights, mix, mix.T, label_table, cotangent, min(8, height)
    )
    grad_table = lax.psum(table_local, ("mp", "dp"))
    rows = reduce(n, parts)
    grad_control = rows[:9].transpose(1, 0, 2).reshape(share, 3, 3, channels)
    return (output, grad_control, rows[9], grad_table)


def solution(mesh):
    in_specs = (
        P(("groups", "dp"), "mp", None, None),
        P(("groups", "dp"), "mp", None),
        P(("groups", "dp")),
        P(),
        P(),
        P("mp", None, None, None),
        P("mp", None, None, None),
        P("mp", None),
        P(("groups", "dp"), "mp", None, None),
    )
    out_specs = (
        P(("groups", "dp"), "mp", None, None),
        P(("groups", "mp"), None, None, None),
        P(("groups", "mp"), None),
        P("groups", None),
    )
    return jax.shard_map(
        functools.partial(per_device, mesh.shape["mp"]),
        mesh=mesh,
        in_specs=in_specs,
        out_specs=out_specs,
        check_vma=False,
    )
```

```python
import functools
import math

import jax
import jax.numpy as jnp
from jax import lax
from jax.experimental import pallas as pl
from jax.experimental.pallas import tpu as pltpu
from jax.sharding import PartitionSpec as P

MESH = pl.DeviceIdType.MESH
LANES = 128
MIB = 1024 * 1024


def ring_position(index, count):
    if count != 8:
        return index
    short, long = index % 2, index // 2
    return (1 - short) * long + short * (count - 1 - long)


def ring_index(position, count):
    if count != 8:
        return position
    short = position // (count // 2)
    long = (1 - short) * position + short * (count - 1 - position)
    return 2 * long + short


def signal_all(targets):
    barrier = pltpu.get_barrier_semaphore()
    for target in targets:
        pl.semaphore_signal(barrier, inc=1, device_id=target, device_id_type=MESH)
    pl.semaphore_wait(barrier, len(targets))


def gather_kernel(
    n, pieces, w_ref, f_ref, e_ref, g_ref, halo_ref, edge_ref,
    ring_send, ring_recv, sib_send, sib_recv, halo_send, halo_recv, own_sem,
):
    me = lax.axis_index("mp")
    core = lax.axis_index("dp")
    pos = ring_position(me, n)
    right = {"mp": ring_index((pos + 1) % n, n)}
    left = {"mp": ring_index((pos + n - 1) % n, n)}
    up = {"mp": (me + n - 1) % n}
    down = {"mp": (me + 1) % n}
    sibling = {"dp": 1 - core}
    signal_all((right, left, up, down, sibling))
    half = w_ref.shape[0] // 2
    size = half // pieces
    rows = f_ref.shape[1]

    def remote(src, dst, send, recv, target):
        return pltpu.make_async_remote_copy(
            src_ref=src, dst_ref=dst, send_sem=send, recv_sem=recv, device_id=target, device_id_type=MESH
        )

    right_steps = n // 2
    left_steps = n - 1 - right_steps
    pending = []
    ring = {}

    def send(side, step, piece):
        shift = n - step if side == 0 else step
        origin = ring_index((pos + shift) % n, n)
        part = pl.ds(core * half + piece * size, size)
        src = w_ref.at[part] if step == 0 else g_ref.at[origin, part]
        slot = side * right_steps + step
        copy = remote(
            src, g_ref.at[origin, part], ring_send.at[slot, piece], ring_recv.at[slot, piece], (right, left)[side]
        )
        copy.start()
        ring[side, step, piece] = copy

    for piece in range(pieces):
        send(0, 0, piece)
        if left_steps:
            send(1, 0, piece)
    edges = [
        remote(f_ref.at[:, rows - 1], halo_ref.at[0], halo_send.at[0], halo_recv.at[0], down),
        remote(f_ref.at[:, 0], halo_ref.at[1], halo_send.at[1], halo_recv.at[1], up),
        remote(e_ref.at[0], edge_ref.at[0], halo_send.at[2], halo_recv.at[2], down),
        remote(e_ref.at[1], edge_ref.at[1], halo_send.at[3], halo_recv.at[3], up),
    ]
    for copy in edges:
        copy.start()
    own = pltpu.make_async_copy(w_ref, g_ref.at[me], own_sem)
    own.start()
    for step in range(right_steps):
        for piece in range(pieces):
            for side, steps in ((0, right_steps), (1, left_steps)):
                if step >= steps:
                    continue
                ring[side, step, piece].wait_recv()
                if step + 1 < steps:
                    send(side, step + 1, piece)
                shift = n - step - 1 if side == 0 else step + 1
                origin = ring_index((pos + shift) % n, n)
                slot = side * right_steps + step
                part = pl.ds(core * half + piece * size, size)
                copy = remote(
                    g_ref.at[origin, part], g_ref.at[origin, part],
                    sib_send.at[slot, piece], sib_recv.at[slot, piece], sibling,
                )
                copy.start()
                pending.append(copy)
    for copy in ring.values():
        copy.wait_send()
    for copy in pending + edges:
        copy.wait()
    own.wait()


def gather(n, w, f, e):
    images, _, depth, span = f.shape
    pieces = 2 if w.shape[0] % 4 == 0 else 1
    return pl.pallas_call(
        functools.partial(gather_kernel, n, pieces),
        out_shape=(
            jax.ShapeDtypeStruct((n,) + w.shape, w.dtype),
            jax.ShapeDtypeStruct((2, images, depth, span), f.dtype),
            jax.ShapeDtypeStruct(e.shape, e.dtype),
        ),
        in_specs=[pl.BlockSpec(memory_space=pl.ANY)] * 3,
        out_specs=(pl.BlockSpec(memory_space=pl.ANY),) * 3,
        scratch_shapes=[
            pltpu.SemaphoreType.DMA((n, pieces)),
            pltpu.SemaphoreType.DMA((n, pieces)),
            pltpu.SemaphoreType.DMA((n, pieces)),
            pltpu.SemaphoreType.DMA((n, pieces)),
            pltpu.SemaphoreType.DMA((4,)),
            pltpu.SemaphoreType.DMA((4,)),
            pltpu.SemaphoreType.DMA,
        ],
        compiler_params=pltpu.CompilerParams(collective_id=0, has_side_effects=True),
        name="gather",
    )(w, f, e)


def compute_kernel(
    n, rows, chunks, lanes, channels, rooms,
    me_ref, main_ref, prev_ref, next_ref, halo_ref, label_ref, edge_ref, shift_ref, w_ref, table_ref, tablet_ref, cot_in_ref,
    out_ref, parts_ref, gtable_ref,
    cols_ref, wide_ref, mix_ref, mixt_ref, cot_ref, grad_ref, gmix_ref,
):
    image = pl.program_id(0)
    chunk = pl.program_id(1)
    first = jnp.logical_and(image == 0, chunk == 0)
    last = jnp.logical_and(image == pl.num_programs(0) - 1, chunk == chunks - 1)
    span = main_ref.shape[3]
    height = rows * chunks

    def weight(tap):
        return w_ref[:, tap].astype(jnp.float32).reshape(channels, channels)

    @pl.when(first)
    def _():
        wide_ref[...] = jnp.zeros_like(wide_ref)
        grad_ref[...] = jnp.zeros_like(grad_ref)
        gmix_ref[...] = jnp.zeros_like(gmix_ref)
        mix_ref[...] = jnp.zeros_like(mix_ref)
        mixt_ref[...] = jnp.zeros_like(mixt_ref)
        mix = weight(9)
        mix_ref[0:channels] = mix.astype(jnp.bfloat16)
        mixt_ref[:, 0:channels] = mix.T.astype(jnp.bfloat16)
        for tap in range(9):
            base = tap * lanes
            control = weight(10 + tap).astype(jnp.bfloat16)
            wide_ref[base : base + channels, 0:channels] = weight(tap).astype(jnp.bfloat16)
            wide_ref[base : base + channels, lanes : lanes + channels] = control
            wide_ref[base + channels : base + channels + rooms, lanes : lanes + channels] = jnp.dot(
                table_ref[...], control, preferred_element_type=jnp.float32
            ).astype(jnp.bfloat16)

    spot = lax.broadcasted_iota(jnp.int32, (span, lanes), 0)
    slot = lax.broadcasted_iota(jnp.int32, (lanes - channels, span), 0)
    for row in range(rows + 2):
        if 0 < row <= rows:
            here = main_ref[0, row - 1]
            label = label_ref[0, pl.ds(chunk * rows + row - 1, 1)]
        else:
            side = 0 if row == 0 else 1
            outside = chunk == (0, chunks - 1)[side]
            dead = jnp.logical_and(outside, me_ref[0] == (0, n - 1)[side])
            beyond = jnp.clip(chunk * rows + row - 1, 0, height - 1)
            here = jnp.where(outside, halo_ref[side, 0], (prev_ref, next_ref)[side][0, 0])
            here = jnp.where(dead, jnp.zeros_like(here), here)
            label = jnp.where(outside, edge_ref[side, 0, 0:1], label_ref[0, pl.ds(beyond, 1)])
            label = jnp.where(dead, -1, label)
        onehot = jnp.where(slot == label, 1.0, 0.0).astype(jnp.bfloat16)
        here = jnp.concatenate([here, onehot], axis=0).T
        wide = here.astype(jnp.float32)
        shifted = (
            jnp.where(spot == 0, 0.0, pltpu.roll(wide, 1, 0)).astype(jnp.bfloat16),
            here,
            jnp.where(spot == span - 1, 0.0, pltpu.roll(wide, span - 1, 0)).astype(jnp.bfloat16),
        )
        for tap_row in range(3):
            spot_row = row - tap_row
            if 0 <= spot_row < rows:
                for tap_col in range(3):
                    base = (tap_row * 3 + tap_col) * lanes
                    cols_ref[spot_row * span : (spot_row + 1) * span, base : base + lanes] = shifted[tap_col]
    for row in range(rows):
        cot_ref[row * span : (row + 1) * span] = cot_in_ref[0, row].T

    cot = cot_ref[...]
    pre = jnp.dot(cols_ref[...], wide_ref[...], preferred_element_type=jnp.float32)
    shift = shift_ref[0]
    trunk = pre[:, :lanes] + shift
    control = pre[:, lanes:] + shift
    gate = 0.5 + 0.5 * jnp.tanh(0.5 * control)
    gated = (control * gate).astype(jnp.bfloat16)
    back = jnp.dot(cot, mixt_ref[...], preferred_element_type=jnp.float32)
    back_pre = (back * gate * (1.0 + control * (1.0 - gate))).astype(jnp.bfloat16)
    mixed = jnp.dot(gated, mix_ref[...], preferred_element_type=jnp.float32)
    trunk = trunk * (0.5 + 0.5 * jnp.tanh(0.5 * trunk))
    out = (trunk[:, :channels] + mixed).astype(jnp.bfloat16)
    for row in range(rows):
        out_ref[0, row] = out[row * span : (row + 1) * span].T
    back_t = back_pre.T[:channels]
    gated_t = gated.T[:channels]
    gmix_ref[...] += jnp.dot(gated_t, cot, preferred_element_type=jnp.float32)
    for tap_row in range(3):
        base = tap_row * 3 * lanes
        grad_ref[:, base : base + 3 * lanes] += jnp.dot(
            back_t, cols_ref[:, base : base + 3 * lanes], preferred_element_type=jnp.float32
        )

    @pl.when(last)
    def _():
        share = channels // n

        def put(tap, block):
            for owner in range(n):
                parts_ref[owner, tap] = block[owner * share : (owner + 1) * share].astype(parts_ref.dtype)

        total = jnp.zeros((2 * rooms, channels), jnp.float32)
        for tap in range(9):
            base = tap * lanes
            block = grad_ref[:, base : base + lanes].T
            room = block[channels : channels + rooms]
            high = room.astype(jnp.bfloat16)
            low = (room - high.astype(jnp.float32)).astype(jnp.bfloat16)
            pair = jnp.concatenate([high, low], axis=0)
            put(tap, block[:channels] + jnp.dot(tablet_ref[...], pair, preferred_element_type=jnp.float32))
            total = total + lax.dot_general(
                pair, wide_ref[base : base + channels, lanes : lanes + channels], (((1,), (1,)), ((), ())),
                preferred_element_type=jnp.float32,
            )
        put(9, gmix_ref[...])
        gtable_ref[...] = total[:rooms] + total[rooms:]


def compute(n, me, latents, halo, labels, edge, shift, weights, table, cotangent, rows, lanes):
    images, height, channels, span = latents.shape
    rooms = table.shape[0]
    chunks = height // rows
    tablet = jnp.concatenate([table.T, table.T], axis=1)

    def whole(array):
        return pl.BlockSpec(array.shape, lambda b, h: (0,) * array.ndim, pipeline_mode=pl.Buffered(1))

    return pl.pallas_call(
        functools.partial(compute_kernel, n, rows, chunks, lanes, channels, rooms),
        grid=(images, chunks),
        out_shape=(
            jax.ShapeDtypeStruct((images, height, channels, span), jnp.bfloat16),
            jax.ShapeDtypeStruct((n, 10, channels // n, channels), jnp.bfloat16),
            jax.ShapeDtypeStruct((rooms, channels), jnp.float32),
        ),
        in_specs=[
            pl.BlockSpec(memory_space=pltpu.SMEM),
            pl.BlockSpec((1, rows, channels, span), lambda b, h: (b, h, 0, 0)),
            pl.BlockSpec((1, 1, channels, span), lambda b, h: (b, jnp.maximum(h * rows - 1, 0), 0, 0)),
            pl.BlockSpec((1, 1, channels, span), lambda b, h: (b, jnp.minimum((h + 1) * rows, height - 1), 0, 0)),
            pl.BlockSpec((2, 1, channels, span), lambda b, h: (0, b, 0, 0)),
            pl.BlockSpec((1, height, span), lambda b, h: (b, 0, 0)),
            pl.BlockSpec((2, 1, 8, span), lambda b, h: (0, b, 0, 0)),
            pl.BlockSpec((1, 1, lanes), lambda b, h: (b, 0, 0)),
            whole(weights),
            whole(table),
            whole(tablet),
            pl.BlockSpec((1, rows, channels, span), lambda b, h: (b, h, 0, 0)),
        ],
        out_specs=(
            pl.BlockSpec((1, rows, channels, span), lambda b, h: (b, h, 0, 0)),
            pl.BlockSpec((n, 10, channels // n, channels), lambda b, h: (0, 0, 0, 0), pipeline_mode=pl.Buffered(1)),
            pl.BlockSpec((rooms, channels), lambda b, h: (0, 0)),
        ),
        scratch_shapes=[
            pltpu.VMEM((rows * span, 9 * lanes), jnp.bfloat16),
            pltpu.VMEM((9 * lanes, 2 * lanes), jnp.bfloat16),
            pltpu.VMEM((lanes, channels), jnp.bfloat16),
            pltpu.VMEM((channels, lanes), jnp.bfloat16),
            pltpu.VMEM((rows * span, channels), jnp.bfloat16),
            pltpu.VMEM((channels, 9 * lanes), jnp.float32),
            pltpu.VMEM((channels, channels), jnp.float32),
        ],
        compiler_params=pltpu.CompilerParams(vmem_limit_bytes=56 * MIB),
        cost_estimate=pl.CostEstimate(flops=60 * 10**9, bytes_accessed=20 * 10**6, transcendentals=4 * 10**6),
        name="convolve",
    )(me, latents, latents, latents, halo, labels, edge, shift, weights, table, tablet, cotangent)


def reduce_kernel(
    n, parts_ref, table_ref, out_ref, sums_ref, other, inbox, outbox, final, table_other, table_both, table_in, table_sum,
    pair_sems, send_sems, recv_sems, last_sems, table_send, table_recv,
):
    me = lax.axis_index("mp")
    core = lax.axis_index("dp")
    pos = ring_position(me, n)
    right = {"mp": ring_index((pos + 1) % n, n)}
    left = {"mp": ring_index((pos + n - 1) % n, n)}
    sibling = {"dp": 1 - core}
    others = [{"mp": (me + step) % n} for step in range(1, n)]
    signal_all(others + [sibling])
    half = parts_ref.shape[1] // 2
    mine = pl.ds(core * half, half)
    theirs = pl.ds((1 - core) * half, half)

    def remote(src, dst, send, recv, target):
        return pltpu.make_async_remote_copy(
            src_ref=src, dst_ref=dst, send_sem=send, recv_sem=recv, device_id=target, device_id_type=MESH
        )

    right_steps = n // 2
    left_steps = n - 1 - right_steps
    order = []
    for step in range(right_steps):
        order.append((0, step))
        if step < left_steps:
            order.append((1, step))

    def goal(side, step):
        if side == 0:
            return ring_index((pos + right_steps - step) % n, n)
        return ring_index((pos + n - left_steps + step) % n, n)

    table_swap = remote(table_ref, table_other, table_send.at[0], table_recv.at[0], sibling)
    table_swap.start()
    pairs = {}
    for spot, key in enumerate(order + [None]):
        owner = me if key is None else goal(*key)
        copy = remote(
            parts_ref.at[owner, theirs], other.at[owner], pair_sems.at[0, spot], pair_sems.at[1, spot], sibling
        )
        copy.start()
        pairs[key] = copy

    table_swap.wait_recv()
    table_both[...] = table_ref[...] + table_other[...]
    table_half = table_ref.shape[0] // 2
    table_mine = pl.ds(pl.multiple_of(core * table_half, table_half), table_half)
    table_in[me] = table_both[table_mine]
    spread = []
    for spot, target in enumerate(others):
        copy = remote(
            table_both.at[table_mine], table_in.at[me], table_send.at[1 + spot], table_recv.at[1 + spot], target
        )
        copy.start()
        spread.append(copy)

    ring = {}
    for side, step in order:
        owner = goal(side, step)
        pairs[side, step].wait_recv()
        total = parts_ref[owner, mine].astype(jnp.float32) + other[owner].astype(jnp.float32)
        slot = side * right_steps + step
        if step:
            ring[side, step - 1].wait_recv()
            total = total + inbox[slot - 1].astype(jnp.float32)
        outbox[slot] = total.astype(outbox.dtype)
        copy = remote(
            outbox.at[slot], inbox.at[slot], send_sems.at[slot], recv_sems.at[slot], (right, left)[side]
        )
        copy.start()
        ring[side, step] = copy
    pairs[None].wait_recv()
    total = parts_ref[me, mine].astype(jnp.float32) + other[me].astype(jnp.float32)
    for side, steps in ((1, left_steps), (0, right_steps)):
        if steps:
            ring[side, steps - 1].wait_recv()
            total = total + inbox[side * right_steps + steps - 1].astype(jnp.float32)
    final[...] = total
    swap = remote(final, out_ref.at[mine], last_sems.at[0], last_sems.at[1], sibling)
    swap.start()
    keep = pltpu.make_async_copy(final, out_ref.at[mine], last_sems.at[2])
    keep.start()
    for spot in range(1, n):
        source = (me + n - spot) % n
        remote(
            table_both.at[table_mine], table_in.at[source], table_send.at[spot], table_recv.at[spot], others[0]
        ).wait_recv()
    table = table_in[0]
    for source in range(1, n):
        table = table + table_in[source]
    table_sum[...] = table
    sums_swap = remote(table_sum, sums_ref.at[table_mine], last_sems.at[3], last_sems.at[4], sibling)
    sums_swap.start()
    sums_keep = pltpu.make_async_copy(table_sum, sums_ref.at[table_mine], last_sems.at[5])
    sums_keep.start()
    table_swap.wait_send()
    for copy in spread:
        copy.wait_send()
    sums_keep.wait()
    sums_swap.wait()
    for copy in pairs.values():
        copy.wait_send()
    for copy in ring.values():
        copy.wait_send()
    keep.wait()
    swap.wait()


def reduce(n, parts, table):
    _, count, share, channels = parts.shape
    half = count // 2
    return pl.pallas_call(
        functools.partial(reduce_kernel, n),
        out_shape=(
            jax.ShapeDtypeStruct((count, share, channels), jnp.float32),
            jax.ShapeDtypeStruct(table.shape, jnp.float32),
        ),
        in_specs=[pl.BlockSpec(memory_space=pltpu.VMEM)] * 2,
        out_specs=(pl.BlockSpec(memory_space=pl.ANY),) * 2,
        scratch_shapes=[
            pltpu.VMEM((n, half, share, channels), jnp.bfloat16),
            pltpu.VMEM((n, half, share, channels), jnp.bfloat16),
            pltpu.VMEM((n, half, share, channels), jnp.bfloat16),
            pltpu.VMEM((half, share, channels), jnp.float32),
            pltpu.VMEM(table.shape, jnp.float32),
            pltpu.VMEM(table.shape, jnp.float32),
            pltpu.VMEM((n, table.shape[0] // 2, channels), jnp.float32),
            pltpu.VMEM((table.shape[0] // 2, channels), jnp.float32),
            pltpu.SemaphoreType.DMA((2, n)),
            pltpu.SemaphoreType.DMA((n,)),
            pltpu.SemaphoreType.DMA((n,)),
            pltpu.SemaphoreType.DMA((6,)),
            pltpu.SemaphoreType.DMA((n,)),
            pltpu.SemaphoreType.DMA((n,)),
        ],
        compiler_params=pltpu.CompilerParams(
            collective_id=1, has_side_effects=True, vmem_limit_bytes=40 * MIB
        ),
        cost_estimate=pl.CostEstimate(flops=10**9, bytes_accessed=50 * 10**6, transcendentals=0),
        name="scatter",
    )(parts, table)


def sinusoid(timesteps, embed_width):
    half_width = embed_width // 2
    indices = jnp.arange(half_width, dtype=jnp.float32)
    frequency = jnp.exp(-math.log(10000.0) * indices / half_width)
    angles = timesteps.astype(jnp.float32)[:, None] * frequency[None, :]
    return jnp.concatenate([jnp.cos(angles), jnp.sin(angles)], axis=1)


def per_device(
    n,
    latents,
    room_labels,
    timesteps,
    label_table,
    time_weight,
    trunk_weight,
    control_weight,
    mix_weight,
    cotangent,
):
    images, height, span, channels = latents.shape
    rooms = label_table.shape[0]
    share = trunk_weight.shape[0]
    lanes = -(-(channels + rooms) // LANES) * LANES
    columns = latents.transpose(0, 1, 3, 2)
    edge_out = jnp.stack([room_labels[:, height - 1], room_labels[:, 0]])
    edge_out = jnp.broadcast_to(edge_out[:, :, None, :], (2, images, 8, span))

    def by_tap(weight):
        return weight.reshape(share, 9, channels).transpose(1, 0, 2)

    packed = jnp.concatenate(
        [by_tap(trunk_weight), mix_weight[None], by_tap(control_weight), mix_weight[None]], axis=0
    )
    gathered, halo, edge = gather(n, packed, columns, edge_out)
    if share % 8:
        gathered = gathered.transpose(1, 0, 2, 3).reshape(1, 20, n * share, channels)
    me = lax.axis_index("mp")[None].astype(jnp.int32)
    time_features = jax.nn.silu(sinusoid(timesteps, time_weight.shape[0])).astype(jnp.bfloat16)
    time_shift = jnp.dot(time_features, time_weight, preferred_element_type=jnp.float32)
    time_shift = jnp.pad(time_shift, ((0, 0), (0, lanes - channels)))[:, None, :]
    output, parts, table_local = compute(
        n, me, columns, halo, room_labels, edge, time_shift, gathered, label_table,
        cotangent.transpose(0, 1, 3, 2), min(8, height), lanes,
    )
    rows, grad_table = reduce(n, parts, table_local)
    output = output.transpose(0, 1, 3, 2)
    grad_control = rows[:9].transpose(1, 0, 2).reshape(share, 3, 3, channels)
    return (output, grad_control, rows[9], grad_table)


def solution(mesh):
    in_specs = (
        P(("groups", "dp"), "mp", None, None),
        P(("groups", "dp"), "mp", None),
        P(("groups", "dp")),
        P(),
        P(),
        P("mp", None, None, None),
        P("mp", None, None, None),
        P("mp", None),
        P(("groups", "dp"), "mp", None, None),
    )
    out_specs = (
        P(("groups", "dp"), "mp", None, None),
        P(("groups", "mp"), None, None, None),
        P(("groups", "mp"), None),
        P("groups", None),
    )
    return jax.shard_map(
        functools.partial(per_device, mesh.shape["mp"]),
        mesh=mesh,
        in_specs=in_specs,
        out_specs=out_specs,
        check_vma=False,
    )
```

```python
import functools
import math

import jax
import jax.numpy as jnp
from jax import lax
from jax.experimental import pallas as pl
from jax.experimental.pallas import tpu as pltpu
from jax.sharding import PartitionSpec as P

MESH = pl.DeviceIdType.MESH
LANES = 128
MIB = 1024 * 1024


def ring_position(index, count):
    if count != 8:
        return index
    short, long = index % 2, index // 2
    return (1 - short) * long + short * (count - 1 - long)


def ring_index(position, count):
    if count != 8:
        return position
    short = position // (count // 2)
    long = (1 - short) * position + short * (count - 1 - position)
    return 2 * long + short


def signal_all(targets):
    barrier = pltpu.get_barrier_semaphore()
    for target in targets:
        pl.semaphore_signal(barrier, inc=1, device_id=target, device_id_type=MESH)
    pl.semaphore_wait(barrier, len(targets))


def gather_kernel(
    n, paired, w_ref, f_ref, e_ref, g_ref, halo_ref, edge_ref,
    ring_send, ring_recv, sib_send, sib_recv, twin_send, twin_recv, halo_send, halo_recv, own_sem,
):
    me = lax.axis_index("mp")
    core = lax.axis_index("dp")
    pos = ring_position(me, n)
    right = {"mp": ring_index((pos + 1) % n, n)}
    left = {"mp": ring_index((pos + n - 1) % n, n)}
    up = {"mp": (me + n - 1) % n}
    down = {"mp": (me + 1) % n}
    sibling = {"dp": 1 - core}
    targets = [right, left, up, down, sibling]
    group = lax.axis_index("groups")
    turn = group % 2
    twin = {"groups": group + 1 - 2 * turn}
    if paired:
        targets.append(twin)
    signal_all(targets)
    half = w_ref.shape[0] // 2
    third = half // 3 if paired else 0
    own_part = pl.ds(core * half + turn * (half - third), third)
    twin_part = pl.ds(core * half + (1 - turn) * (half - third), third)
    shared_part = pl.ds(core * half + third, half - 2 * third)
    parts = (own_part, shared_part) if paired else (shared_part,)
    pieces = len(parts)
    rows = f_ref.shape[1]

    def remote(src, dst, send, recv, target):
        return pltpu.make_async_remote_copy(
            src_ref=src, dst_ref=dst, send_sem=send, recv_sem=recv, device_id=target, device_id_type=MESH
        )

    right_steps = n // 2
    left_steps = n - 1 - right_steps
    pending = []
    ring = {}

    def send(side, step, piece):
        shift = n - step if side == 0 else step
        origin = ring_index((pos + shift) % n, n)
        part = parts[piece]
        src = w_ref.at[part] if step == 0 else g_ref.at[origin, part]
        slot = side * right_steps + step
        copy = remote(
            src, g_ref.at[origin, part], ring_send.at[slot, piece], ring_recv.at[slot, piece], (right, left)[side]
        )
        copy.start()
        ring[side, step, piece] = copy

    sent = []
    arriving = []

    def pass_on(count):
        for slot, origin in arriving[:count]:
            block = g_ref.at[origin, twin_part]
            remote(block, block, twin_send.at[slot], twin_recv.at[slot], twin).wait_recv()
            copy = remote(block, block, sib_send.at[slot, 2], sib_recv.at[slot, 2], sibling)
            copy.start()
            pending.append(copy)
        del arriving[:count]

    for piece in range(pieces):
        send(0, 0, piece)
        if left_steps:
            send(1, 0, piece)
    edges = [
        remote(f_ref.at[:, rows - 1], halo_ref.at[0], halo_send.at[0], halo_recv.at[0], down),
        remote(f_ref.at[:, 0], halo_ref.at[1], halo_send.at[1], halo_recv.at[1], up),
        remote(e_ref.at[0], edge_ref.at[0], halo_send.at[2], halo_recv.at[2], down),
        remote(e_ref.at[1], edge_ref.at[1], halo_send.at[3], halo_recv.at[3], up),
    ]
    for copy in edges:
        copy.start()
    own = pltpu.make_async_copy(w_ref, g_ref.at[me], own_sem)
    own.start()
    for step in range(right_steps):
        for piece in range(pieces):
            for side, steps in ((0, right_steps), (1, left_steps)):
                if step >= steps:
                    continue
                ring[side, step, piece].wait_recv()
                if step + 1 < steps:
                    send(side, step + 1, piece)
                shift = n - step - 1 if side == 0 else step + 1
                origin = ring_index((pos + shift) % n, n)
                slot = side * right_steps + step
                part = parts[piece]
                if paired and piece == 0:
                    copy = remote(
                        g_ref.at[origin, part], g_ref.at[origin, part], twin_send.at[slot], twin_recv.at[slot], twin
                    )
                    copy.start()
                    sent.append(copy)
                    arriving.append((slot, origin))
                copy = remote(
                    g_ref.at[origin, part], g_ref.at[origin, part],
                    sib_send.at[slot, piece], sib_recv.at[slot, piece], sibling,
                )
                copy.start()
                pending.append(copy)
        if step:
            pass_on(2 if step < left_steps + 1 else 1)
    pass_on(len(arriving))
    for copy in sent:
        copy.wait_send()
    for copy in ring.values():
        copy.wait_send()
    for copy in pending + edges:
        copy.wait()
    own.wait()


def gather(n, groups, w, f, e):
    images, _, depth, span = f.shape
    return pl.pallas_call(
        functools.partial(gather_kernel, n, groups % 2 == 0),
        out_shape=(
            jax.ShapeDtypeStruct((n,) + w.shape, w.dtype),
            jax.ShapeDtypeStruct((2, images, depth, span), f.dtype),
            jax.ShapeDtypeStruct(e.shape, e.dtype),
        ),
        in_specs=[pl.BlockSpec(memory_space=pl.ANY)] * 3,
        out_specs=(pl.BlockSpec(memory_space=pl.ANY),) * 3,
        scratch_shapes=[
            pltpu.SemaphoreType.DMA((n, 2)),
            pltpu.SemaphoreType.DMA((n, 2)),
            pltpu.SemaphoreType.DMA((n, 3)),
            pltpu.SemaphoreType.DMA((n, 3)),
            pltpu.SemaphoreType.DMA((n,)),
            pltpu.SemaphoreType.DMA((n,)),
            pltpu.SemaphoreType.DMA((4,)),
            pltpu.SemaphoreType.DMA((4,)),
            pltpu.SemaphoreType.DMA,
        ],
        compiler_params=pltpu.CompilerParams(collective_id=0, has_side_effects=True),
        name="gather",
    )(w, f, e)


def compute_kernel(
    n, rows, chunks, lanes, channels, rooms,
    me_ref, main_ref, prev_ref, next_ref, halo_ref, label_ref, edge_ref, shift_ref, w_ref, table_ref, tablet_ref, cot_in_ref,
    out_ref, parts_ref, gtable_ref,
    cols_ref, wide_ref, mix_ref, mixt_ref, cot_ref, grad_ref, gmix_ref,
):
    image = pl.program_id(0)
    chunk = pl.program_id(1)
    first = jnp.logical_and(image == 0, chunk == 0)
    last = jnp.logical_and(image == pl.num_programs(0) - 1, chunk == chunks - 1)
    span = main_ref.shape[3]
    height = rows * chunks

    def weight(tap):
        return w_ref[:, tap].astype(jnp.float32).reshape(channels, channels)

    @pl.when(first)
    def _():
        wide_ref[...] = jnp.zeros_like(wide_ref)
        grad_ref[...] = jnp.zeros_like(grad_ref)
        gmix_ref[...] = jnp.zeros_like(gmix_ref)
        mix_ref[...] = jnp.zeros_like(mix_ref)
        mixt_ref[...] = jnp.zeros_like(mixt_ref)
        mix = weight(9)
        mix_ref[0:channels] = mix.astype(jnp.bfloat16)
        mixt_ref[:, 0:channels] = mix.T.astype(jnp.bfloat16)
        for tap in range(9):
            base = tap * lanes
            control = weight(10 + tap).astype(jnp.bfloat16)
            wide_ref[base : base + channels, 0:channels] = weight(tap).astype(jnp.bfloat16)
            wide_ref[base : base + channels, lanes : lanes + channels] = control
            wide_ref[base + channels : base + channels + rooms, lanes : lanes + channels] = jnp.dot(
                table_ref[...], control, preferred_element_type=jnp.float32
            ).astype(jnp.bfloat16)

    spot = lax.broadcasted_iota(jnp.int32, (span, lanes), 0)
    slot = lax.broadcasted_iota(jnp.int32, (lanes - channels, span), 0)
    for row in range(rows + 2):
        if 0 < row <= rows:
            here = main_ref[0, row - 1]
            label = label_ref[0, pl.ds(chunk * rows + row - 1, 1)]
        else:
            side = 0 if row == 0 else 1
            outside = chunk == (0, chunks - 1)[side]
            dead = jnp.logical_and(outside, me_ref[0] == (0, n - 1)[side])
            beyond = jnp.clip(chunk * rows + row - 1, 0, height - 1)
            here = jnp.where(outside, halo_ref[side, 0], (prev_ref, next_ref)[side][0, 0])
            here = jnp.where(dead, jnp.zeros_like(here), here)
            label = jnp.where(outside, edge_ref[side, 0, 0:1], label_ref[0, pl.ds(beyond, 1)])
            label = jnp.where(dead, -1, label)
        onehot = jnp.where(slot == label, 1.0, 0.0).astype(jnp.bfloat16)
        here = jnp.concatenate([here, onehot], axis=0).T
        wide = here.astype(jnp.float32)
        shifted = (
            jnp.where(spot == 0, 0.0, pltpu.roll(wide, 1, 0)).astype(jnp.bfloat16),
            here,
            jnp.where(spot == span - 1, 0.0, pltpu.roll(wide, span - 1, 0)).astype(jnp.bfloat16),
        )
        for tap_row in range(3):
            spot_row = row - tap_row
            if 0 <= spot_row < rows:
                for tap_col in range(3):
                    base = (tap_row * 3 + tap_col) * lanes
                    cols_ref[spot_row * span : (spot_row + 1) * span, base : base + lanes] = shifted[tap_col]
    for row in range(rows):
        cot_ref[row * span : (row + 1) * span] = cot_in_ref[0, row].T

    cot = cot_ref[...]
    pre = jnp.dot(cols_ref[...], wide_ref[...], preferred_element_type=jnp.float32)
    shift = shift_ref[0]
    trunk = pre[:, :lanes] + shift
    control = pre[:, lanes:] + shift
    gate = 0.5 + 0.5 * jnp.tanh(0.5 * control)
    gated = (control * gate).astype(jnp.bfloat16)
    back = jnp.dot(cot, mixt_ref[...], preferred_element_type=jnp.float32)
    back_pre = (back * gate * (1.0 + control * (1.0 - gate))).astype(jnp.bfloat16)
    mixed = jnp.dot(gated, mix_ref[...], preferred_element_type=jnp.float32)
    trunk = trunk * (0.5 + 0.5 * jnp.tanh(0.5 * trunk))
    out = (trunk[:, :channels] + mixed).astype(jnp.bfloat16)
    for row in range(rows):
        out_ref[0, row] = out[row * span : (row + 1) * span].T
    back_t = back_pre.T[:channels]
    gated_t = gated.T[:channels]
    gmix_ref[...] += jnp.dot(gated_t, cot, preferred_element_type=jnp.float32)
    for tap_row in range(3):
        base = tap_row * 3 * lanes
        grad_ref[:, base : base + 3 * lanes] += jnp.dot(
            back_t, cols_ref[:, base : base + 3 * lanes], preferred_element_type=jnp.float32
        )

    @pl.when(last)
    def _():
        share = channels // n

        def put(tap, block):
            for owner in range(n):
                parts_ref[owner, tap] = block[owner * share : (owner + 1) * share].astype(parts_ref.dtype)

        total = jnp.zeros((2 * rooms, channels), jnp.float32)
        for tap in range(9):
            base = tap * lanes
            block = grad_ref[:, base : base + lanes].T
            room = block[channels : channels + rooms]
            high = room.astype(jnp.bfloat16)
            low = (room - high.astype(jnp.float32)).astype(jnp.bfloat16)
            pair = jnp.concatenate([high, low], axis=0)
            put(tap, block[:channels] + jnp.dot(tablet_ref[...], pair, preferred_element_type=jnp.float32))
            total = total + lax.dot_general(
                pair, wide_ref[base : base + channels, lanes : lanes + channels], (((1,), (1,)), ((), ())),
                preferred_element_type=jnp.float32,
            )
        put(9, gmix_ref[...])
        gtable_ref[...] = total[:rooms] + total[rooms:]


def compute(n, me, latents, halo, labels, edge, shift, weights, table, cotangent, rows, lanes):
    images, height, channels, span = latents.shape
    rooms = table.shape[0]
    chunks = height // rows
    tablet = jnp.concatenate([table.T, table.T], axis=1)

    def whole(array):
        return pl.BlockSpec(array.shape, lambda b, h: (0,) * array.ndim, pipeline_mode=pl.Buffered(1))

    return pl.pallas_call(
        functools.partial(compute_kernel, n, rows, chunks, lanes, channels, rooms),
        grid=(images, chunks),
        out_shape=(
            jax.ShapeDtypeStruct((images, height, channels, span), jnp.bfloat16),
            jax.ShapeDtypeStruct((n, 10, channels // n, channels), jnp.bfloat16),
            jax.ShapeDtypeStruct((rooms, channels), jnp.float32),
        ),
        in_specs=[
            pl.BlockSpec(memory_space=pltpu.SMEM),
            pl.BlockSpec((1, rows, channels, span), lambda b, h: (b, h, 0, 0)),
            pl.BlockSpec((1, 1, channels, span), lambda b, h: (b, jnp.maximum(h * rows - 1, 0), 0, 0)),
            pl.BlockSpec((1, 1, channels, span), lambda b, h: (b, jnp.minimum((h + 1) * rows, height - 1), 0, 0)),
            pl.BlockSpec((2, 1, channels, span), lambda b, h: (0, b, 0, 0)),
            pl.BlockSpec((1, height, span), lambda b, h: (b, 0, 0)),
            pl.BlockSpec((2, 1, 8, span), lambda b, h: (0, b, 0, 0)),
            pl.BlockSpec((1, 1, lanes), lambda b, h: (b, 0, 0)),
            whole(weights),
            whole(table),
            whole(tablet),
            pl.BlockSpec((1, rows, channels, span), lambda b, h: (b, h, 0, 0)),
        ],
        out_specs=(
            pl.BlockSpec((1, rows, channels, span), lambda b, h: (b, h, 0, 0)),
            pl.BlockSpec((n, 10, channels // n, channels), lambda b, h: (0, 0, 0, 0), pipeline_mode=pl.Buffered(1)),
            pl.BlockSpec((rooms, channels), lambda b, h: (0, 0)),
        ),
        scratch_shapes=[
            pltpu.VMEM((rows * span, 9 * lanes), jnp.bfloat16),
            pltpu.VMEM((9 * lanes, 2 * lanes), jnp.bfloat16),
            pltpu.VMEM((lanes, channels), jnp.bfloat16),
            pltpu.VMEM((channels, lanes), jnp.bfloat16),
            pltpu.VMEM((rows * span, channels), jnp.bfloat16),
            pltpu.VMEM((channels, 9 * lanes), jnp.float32),
            pltpu.VMEM((channels, channels), jnp.float32),
        ],
        compiler_params=pltpu.CompilerParams(vmem_limit_bytes=56 * MIB),
        cost_estimate=pl.CostEstimate(flops=60 * 10**9, bytes_accessed=20 * 10**6, transcendentals=4 * 10**6),
        name="convolve",
    )(me, latents, latents, latents, halo, labels, edge, shift, weights, table, tablet, cotangent)


def reduce_kernel(
    n, parts_ref, table_ref, out_ref, sums_ref, other, inbox, outbox, final, table_other, table_both, table_in, table_sum,
    pair_sems, send_sems, recv_sems, last_sems, table_send, table_recv,
):
    me = lax.axis_index("mp")
    core = lax.axis_index("dp")
    pos = ring_position(me, n)
    right = {"mp": ring_index((pos + 1) % n, n)}
    left = {"mp": ring_index((pos + n - 1) % n, n)}
    sibling = {"dp": 1 - core}
    others = [{"mp": (me + step) % n} for step in range(1, n)]
    signal_all(others + [sibling])
    half = parts_ref.shape[1] // 2
    mine = pl.ds(core * half, half)
    theirs = pl.ds((1 - core) * half, half)

    def remote(src, dst, send, recv, target):
        return pltpu.make_async_remote_copy(
            src_ref=src, dst_ref=dst, send_sem=send, recv_sem=recv, device_id=target, device_id_type=MESH
        )

    right_steps = n // 2
    left_steps = n - 1 - right_steps
    order = []
    for step in range(right_steps):
        order.append((0, step))
        if step < left_steps:
            order.append((1, step))

    def goal(side, step):
        if side == 0:
            return ring_index((pos + right_steps - step) % n, n)
        return ring_index((pos + n - left_steps + step) % n, n)

    table_swap = remote(table_ref, table_other, table_send.at[0], table_recv.at[0], sibling)
    table_swap.start()
    pairs = {}
    for spot, key in enumerate(order + [None]):
        owner = me if key is None else goal(*key)
        copy = remote(
            parts_ref.at[owner, theirs], other.at[owner], pair_sems.at[0, spot], pair_sems.at[1, spot], sibling
        )
        copy.start()
        pairs[key] = copy

    table_swap.wait_recv()
    table_both[...] = table_ref[...] + table_other[...]
    table_half = table_ref.shape[0] // 2
    table_mine = pl.ds(pl.multiple_of(core * table_half, table_half), table_half)
    table_in[me] = table_both[table_mine]
    spread = []
    for spot, target in enumerate(others):
        copy = remote(
            table_both.at[table_mine], table_in.at[me], table_send.at[1 + spot], table_recv.at[1 + spot], target
        )
        copy.start()
        spread.append(copy)

    ring = {}
    for side, step in order:
        owner = goal(side, step)
        pairs[side, step].wait_recv()
        total = parts_ref[owner, mine].astype(jnp.float32) + other[owner].astype(jnp.float32)
        slot = side * right_steps + step
        if step:
            ring[side, step - 1].wait_recv()
            total = total + inbox[slot - 1].astype(jnp.float32)
        outbox[slot] = total.astype(outbox.dtype)
        copy = remote(
            outbox.at[slot], inbox.at[slot], send_sems.at[slot], recv_sems.at[slot], (right, left)[side]
        )
        copy.start()
        ring[side, step] = copy
    pairs[None].wait_recv()
    total = parts_ref[me, mine].astype(jnp.float32) + other[me].astype(jnp.float32)
    for side, steps in ((1, left_steps), (0, right_steps)):
        if steps:
            ring[side, steps - 1].wait_recv()
            total = total + inbox[side * right_steps + steps - 1].astype(jnp.float32)
    final[...] = total
    swap = remote(final, out_ref.at[mine], last_sems.at[0], last_sems.at[1], sibling)
    swap.start()
    keep = pltpu.make_async_copy(final, out_ref.at[mine], last_sems.at[2])
    keep.start()
    for spot in range(1, n):
        source = (me + n - spot) % n
        remote(
            table_both.at[table_mine], table_in.at[source], table_send.at[spot], table_recv.at[spot], others[0]
        ).wait_recv()
    table = table_in[0]
    for source in range(1, n):
        table = table + table_in[source]
    table_sum[...] = table
    sums_swap = remote(table_sum, sums_ref.at[table_mine], last_sems.at[3], last_sems.at[4], sibling)
    sums_swap.start()
    sums_keep = pltpu.make_async_copy(table_sum, sums_ref.at[table_mine], last_sems.at[5])
    sums_keep.start()
    table_swap.wait_send()
    for copy in spread:
        copy.wait_send()
    sums_keep.wait()
    sums_swap.wait()
    for copy in pairs.values():
        copy.wait_send()
    for copy in ring.values():
        copy.wait_send()
    keep.wait()
    swap.wait()


def reduce(n, parts, table):
    _, count, share, channels = parts.shape
    half = count // 2
    return pl.pallas_call(
        functools.partial(reduce_kernel, n),
        out_shape=(
            jax.ShapeDtypeStruct((count, share, channels), jnp.float32),
            jax.ShapeDtypeStruct(table.shape, jnp.float32),
        ),
        in_specs=[pl.BlockSpec(memory_space=pltpu.VMEM)] * 2,
        out_specs=(pl.BlockSpec(memory_space=pl.ANY),) * 2,
        scratch_shapes=[
            pltpu.VMEM((n, half, share, channels), jnp.bfloat16),
            pltpu.VMEM((n, half, share, channels), jnp.bfloat16),
            pltpu.VMEM((n, half, share, channels), jnp.bfloat16),
            pltpu.VMEM((half, share, channels), jnp.float32),
            pltpu.VMEM(table.shape, jnp.float32),
            pltpu.VMEM(table.shape, jnp.float32),
            pltpu.VMEM((n, table.shape[0] // 2, channels), jnp.float32),
            pltpu.VMEM((table.shape[0] // 2, channels), jnp.float32),
            pltpu.SemaphoreType.DMA((2, n)),
            pltpu.SemaphoreType.DMA((n,)),
            pltpu.SemaphoreType.DMA((n,)),
            pltpu.SemaphoreType.DMA((6,)),
            pltpu.SemaphoreType.DMA((n,)),
            pltpu.SemaphoreType.DMA((n,)),
        ],
        compiler_params=pltpu.CompilerParams(
            collective_id=1, has_side_effects=True, vmem_limit_bytes=40 * MIB
        ),
        cost_estimate=pl.CostEstimate(flops=10**9, bytes_accessed=50 * 10**6, transcendentals=0),
        name="scatter",
    )(parts, table)


def sinusoid(timesteps, embed_width):
    half_width = embed_width // 2
    indices = jnp.arange(half_width, dtype=jnp.float32)
    frequency = jnp.exp(-math.log(10000.0) * indices / half_width)
    angles = timesteps.astype(jnp.float32)[:, None] * frequency[None, :]
    return jnp.concatenate([jnp.cos(angles), jnp.sin(angles)], axis=1)


def per_device(
    n,
    groups,
    latents,
    room_labels,
    timesteps,
    label_table,
    time_weight,
    trunk_weight,
    control_weight,
    mix_weight,
    cotangent,
):
    images, height, span, channels = latents.shape
    rooms = label_table.shape[0]
    share = trunk_weight.shape[0]
    lanes = -(-(channels + rooms) // LANES) * LANES
    columns = latents.transpose(0, 1, 3, 2)
    edge_out = jnp.stack([room_labels[:, height - 1], room_labels[:, 0]])
    edge_out = jnp.broadcast_to(edge_out[:, :, None, :], (2, images, 8, span))

    def by_tap(weight):
        return weight.reshape(share, 9, channels).transpose(1, 0, 2)

    packed = jnp.concatenate(
        [by_tap(trunk_weight), mix_weight[None], by_tap(control_weight), mix_weight[None]], axis=0
    )
    gathered, halo, edge = gather(n, groups, packed, columns, edge_out)
    if share % 8:
        gathered = gathered.transpose(1, 0, 2, 3).reshape(1, 20, n * share, channels)
    me = lax.axis_index("mp")[None].astype(jnp.int32)
    time_features = jax.nn.silu(sinusoid(timesteps, time_weight.shape[0])).astype(jnp.bfloat16)
    time_shift = jnp.dot(time_features, time_weight, preferred_element_type=jnp.float32)
    time_shift = jnp.pad(time_shift, ((0, 0), (0, lanes - channels)))[:, None, :]
    output, parts, table_local = compute(
        n, me, columns, halo, room_labels, edge, time_shift, gathered, label_table,
        cotangent.transpose(0, 1, 3, 2), min(8, height), lanes,
    )
    rows, grad_table = reduce(n, parts, table_local)
    output = output.transpose(0, 1, 3, 2)
    grad_control = rows[:9].transpose(1, 0, 2).reshape(share, 3, 3, channels)
    return (output, grad_control, rows[9], grad_table)


def solution(mesh):
    in_specs = (
        P(("groups", "dp"), "mp", None, None),
        P(("groups", "dp"), "mp", None),
        P(("groups", "dp")),
        P(),
        P(),
        P("mp", None, None, None),
        P("mp", None, None, None),
        P("mp", None),
        P(("groups", "dp"), "mp", None, None),
    )
    out_specs = (
        P(("groups", "dp"), "mp", None, None),
        P(("groups", "mp"), None, None, None),
        P(("groups", "mp"), None),
        P("groups", None),
    )
    return jax.shard_map(
        functools.partial(per_device, mesh.shape["mp"], mesh.shape["groups"]),
        mesh=mesh,
        in_specs=in_specs,
        out_specs=out_specs,
        check_vma=False,
    )
```
